128 devices in a mesh: basis: 8 (over y, x_hi), aux: 16 (over x_lo, z, core).
Axes of the slice: x: 4 (x_hi: 2, x_lo: 2; x = x_hi * 2 + x_lo), y: 4, z: 4, core: 2. Of those that a mesh axis runs over, the one named last changes fastest.
Arguments:
- half_ints: bfloat16 [2, 8000, 24000], P(None, 'basis', 'aux'), may hold values from -6 to 6
- virt_coeffs: bfloat16 [8000, 768], P('basis'), may hold values from -0.0625 to 0.0625
- metric_factor: bfloat16 [24000, 24000], P('aux', 'basis'), as said below
Outputs:
- fitted: float32 [1536, 24000], P('aux', 'basis')
The draws below stay inside these ranges and needn't reach their ends.
Inputs may be any that keep to these rules, and one draw needn't show every extreme that they name: metric_factor is zero where the row index exceeds the column index; its diagonal is positive.
All inputs are finite; a program needn't handle non-finite values.
Results may differ from the reference program's by a relative error of at most 0.0029.
Values may be sent and summed in bfloat16 or wider, within the bound.
No kernel may reach another device: no remote copies, remote signals or barrier semaphores. Data moves between devices by JAX's collectives and lax.ppermute only.
A program may use at most 128 MiB of HBM per device.

```python
import jax
import jax.numpy as jnp
from jax import lax

NB = 8000
NAUX = 24000
NOCC = 2
NVIR = 768


def draw_metric_factor(key, part):
    key = jax.random.fold_in(key, 7)
    noise_key, diag_key = jax.random.split(key)
    noise = jax.random.normal(noise_key, (NAUX, NAUX), jnp.float32)
    diag = jax.random.uniform(diag_key, (NAUX,), jnp.float32, 0.5, 1.5)
    rows = jnp.arange(NAUX)[:, None]
    cols = jnp.arange(NAUX)[None, :]
    upper = jnp.where(rows < cols, noise * (0.8 / jnp.sqrt(jnp.float32(NAUX))), 0.0)
    full = upper + jnp.where(rows == cols, diag[:, None], 0.0)
    return full.astype(jnp.bfloat16)


def block_scale(stream_key, dims, pieces, least, high):
    def one(position, shards_of):
        draws = jax.random.uniform(jax.random.fold_in(jax.random.fold_in(stream_key, 6), position), (shards_of,), jnp.float32, least / len(pieces), high / len(pieces))
        return jnp.repeat(jnp.exp(draws), dims[position] // shards_of).reshape((-1,) + (1,) * (len(dims) - position - 1))

    factor_of = one(*pieces[0])
    for cut in pieces[1:]:
        factor_of = factor_of * one(*cut)
    return factor_of


def bell_draw(rng, dims, spread, limit, pieces=(), dtype=jnp.bfloat16):
    level = block_scale(rng, dims, pieces, -0.22, 0.18) if pieces else 1.0
    array = jax.random.normal(rng, dims, jnp.float32) * spread * level
    return jnp.minimum(jnp.maximum(array, -limit), limit).astype(dtype)


def setup_inputs(seed: int = 0) -> dict:
    seeds = jax.random.split(jax.random.key(seed), 4)
    half_ints = bell_draw(seeds[0], (NOCC, NB, NAUX), 1.0, 6.0, ((1, 8), (2, 16)))
    virt_coeffs = bell_draw(seeds[1], (NB, NVIR), NB ** -0.5, 0.0625, ((0, 8),))
    metric_factor = draw_metric_factor(jax.random.fold_in(seeds[3], 71), 0)
    return {"half_ints": half_ints, "virt_coeffs": virt_coeffs, "metric_factor": metric_factor}


def reference(half_ints, virt_coeffs, metric_factor):
    blocks = []
    for occ in range(NOCC):
        blocks.append(lax.dot_general(virt_coeffs, half_ints[occ], (((0,), (0,)), ((), ())), preferred_element_type=jnp.float32))
    stacked = jnp.stack(blocks, axis=1)
    pair_ints = stacked.reshape(NVIR * NOCC, stacked.shape[2]).astype(jnp.bfloat16)
    fitted = jnp.dot(pair_ints, metric_factor, preferred_element_type=jnp.float32)
    return fitted
```

```python
import jax
import jax.numpy as jnp
from jax import lax
from jax.sharding import PartitionSpec as P

NY, NH, NL, NZ, NC = 4, 2, 2, 4, 2
PARTS = (4, 4, 4)
STEPS = (1, 2, 3, 0)
SCALE = 16.0


def ring_y(step):
    return [(y * NH + h, (y + step) % NY * NH + h) for y in range(NY) for h in range(NH)]


def ring_z(step):
    return [
        ((l * NZ + z) * NC + k, (l * NZ + (z + step) % NZ) * NC + k)
        for l in range(NL)
        for z in range(NZ)
        for k in range(NC)
    ]


SWAP_H = [(i, i ^ 1) for i in range(NY * NH)]
SWAP_CORE = [(i, i ^ 1) for i in range(NL * NZ * NC)]
SWAP_L = [(i, i ^ (NZ * NC)) for i in range(NL * NZ * NC)]


def on_y(x, step):
    return lax.ppermute(x, "basis", ring_y(step))


def on_z(x, step):
    return lax.ppermute(x, "aux", ring_z(step))


def places():
    basis, aux = lax.axis_index("basis"), lax.axis_index("aux")
    return basis // NH, aux // (NZ * NC), aux // NC % NZ, aux % NC


def column_order(quarter):
    y, l, z, k = places()
    steps = jnp.array(STEPS)
    order, start = [], 0
    for rows in PARTS:
        u = (y + steps) % NY
        target = ((l ^ jnp.array([1, 0]))[None, None, :] * NZ + ((z + steps) % NZ)[None, :, None]) * NC
        target = target + (k ^ jnp.array([0, 1]))[:, None, None]
        first = target[None] * (NY * quarter) + u[:, None, None, None] * quarter + start
        order.append((first[..., None] + jnp.arange(rows)).reshape(-1))
        start += rows
    return jnp.concatenate(order)


def row_order(quarter, n_occ):
    y = places()[0]
    j = jnp.arange(NY * quarter)[:, None]
    i = jnp.arange(n_occ)[None, :]
    step = (j // quarter - y) % NY
    slot = jnp.zeros_like(step)
    for n, s in enumerate(STEPS):
        slot = jnp.where(step == s, n, slot)
    r = j % quarter
    place, start = jnp.zeros_like(j + i), 0
    for rows in PARTS:
        here = start * NY * n_occ + (slot * n_occ + i) * rows + r - start
        place = jnp.where((r >= start) & (r < start + rows), here, place)
        start += rows
    return place.reshape(-1)


def f32(x):
    return x.astype(jnp.float32)


def pair_sums(half_ints, cols, rows):
    n_occ, _, width = half_ints.shape
    per = NC * NZ * NL * rows
    blocks = [
        (lax.dot_general(cols, half_ints[i], (((0,), (0,)), ((), ())), preferred_element_type=jnp.float32) * SCALE)
        .astype(jnp.float16)
        .reshape(NY, per, width)
        for i in range(n_occ)
    ]
    near, far, back, mine = [[blocks[i][n] for i in range(n_occ)] for n in range(NY)]
    add_near = on_y(far[0], 1)
    add_back = on_y(far[1], 3)
    near = jnp.stack([(f32(near[0]) + f32(add_near)).astype(jnp.float16), near[1]])
    back = jnp.stack([back[0], (f32(back[1]) + f32(add_back)).astype(jnp.float16)])
    total = f32(jnp.stack(mine)) + f32(on_y(near, 1)) + f32(on_y(back, 3))
    other = lax.ppermute(total.astype(jnp.float16), "basis", SWAP_H)
    pair = ((total + f32(other)) * (1 / SCALE)).astype(jnp.bfloat16)
    keep = per // NC
    swapped = lax.ppermute(pair[:, keep:], "aux", SWAP_CORE)
    block = jnp.stack([pair[:, :keep], swapped], axis=1)
    from_left, from_right = on_y(block, 1), on_y(block, 3)
    opposite = jnp.stack([on_y(from_left[0], 1), on_y(from_right[1], 3)])
    return [from_right, opposite, from_left, block]


def reduce_rows(units, rows):
    near, far, back, mine = units
    half = far.shape[0] // 2
    b16 = lambda x: x.astype(jnp.bfloat16)
    add_near = on_z(b16(far[:half]), 1)
    add_back = on_z(b16(far[half:]), 3)
    near = jnp.concatenate([b16(near[:half] + f32(add_near)), b16(near[half:])])
    back = jnp.concatenate([b16(back[:half]), b16(back[half:] + f32(add_back))])
    total = mine + f32(on_z(near, 1)) + f32(on_z(back, 3))
    other = lax.ppermute(b16(total[:, :, 0]), "aux", SWAP_L)
    return total[:, :, 1] + f32(other)


def on_device(half_ints, virt_coeffs, metric_factor):
    n_occ = half_ints.shape[0]
    n_vir = virt_coeffs.shape[1]
    width = metric_factor.shape[1]
    quarter = n_vir // (NL * NZ * NC * NY)
    other_factor = lax.ppermute(metric_factor, "aux", SWAP_CORE)
    pick = (jnp.arange(n_vir)[:, None] == column_order(quarter)[None, :]).astype(jnp.bfloat16)
    cols = jnp.dot(virt_coeffs, pick, preferred_element_type=jnp.float32).astype(jnp.bfloat16)
    results, start = [], 0
    for rows in PARTS:
        size = NY * NC * NZ * NL * rows
        units = pair_sums(half_ints, cols[:, start : start + size], rows)
        start += size
        block = jnp.stack(units)
        block = block.transpose(2, 0, 1, 3, 4).reshape(2, NY * n_occ * NZ * NL * rows, -1)
        fitted = jnp.dot(block[0], metric_factor, preferred_element_type=jnp.float32)
        fitted = fitted + jnp.dot(block[1], other_factor, preferred_element_type=jnp.float32)
        fitted = fitted.reshape(NY, n_occ, NZ, NL, rows, width)
        done = reduce_rows([fitted[:, :, n] for n in range(NZ)], rows)
        results.append(done.reshape(NY * n_occ * rows, width))
    results = jnp.concatenate(results)
    place = (row_order(quarter, n_occ)[:, None] == jnp.arange(results.shape[0])[None, :]).astype(jnp.float32)
    return jnp.dot(place, results, precision=lax.Precision.HIGHEST, preferred_element_type=jnp.float32)


def solution(mesh):
    placed = (P(None, "basis", "aux"), P("basis", None), P("aux", "basis"))
    return jax.shard_map(
        on_device, mesh=mesh, in_specs=placed, out_specs=P("aux", "basis"), check_vma=False
    )
```

```python
import jax
import jax.numpy as jnp
from jax import lax
from jax.experimental import pallas as pl
from jax.experimental.pallas import tpu as pltpu
from jax.sharding import PartitionSpec as P

NY, NH, NL, NZ, NC = 4, 2, 2, 4, 2
PARTS = (4, 4, 4)
SCALE = 16.0
TILE = 512

SWAP_H = [(i, i ^ 1) for i in range(NY * NH)]
SWAP_CORE = [(i, i ^ 1) for i in range(NL * NZ * NC)]
SWAP_L = [(i, i ^ (NZ * NC)) for i in range(NL * NZ * NC)]


def on_y(x, step):
    pairs = [(y * NH + h, (y + step) % NY * NH + h) for y in range(NY) for h in range(NH)]
    return lax.ppermute(x, "basis", pairs)


def on_z(x, step):
    pairs = [
        ((l * NZ + z) * NC + k, (l * NZ + (z + step) % NZ) * NC + k)
        for l in range(NL)
        for z in range(NZ)
        for k in range(NC)
    ]
    return lax.ppermute(x, "aux", pairs)


def places():
    basis, aux = lax.axis_index("basis"), lax.axis_index("aux")
    return basis // NH, aux // (NZ * NC), aux // NC % NZ, aux % NC


def after(x, earlier):
    return lax.optimization_barrier((x, earlier))[0]


def f32(x):
    return x.astype(jnp.float32)


def b16(x):
    return x.astype(jnp.bfloat16)


def picked(virt_coeffs, quarter, start, rows):
    y, l, z, k = places()
    n_vir = virt_coeffs.shape[1]
    size = NY * NC * NZ * NL * rows
    at = lax.broadcasted_iota(jnp.int32, (n_vir, size), 1)
    r, at = at % rows, at // rows
    ll, at = at % NL, at // NL
    zz, at = at % NZ, at // NZ
    kk, yy = at % NC, at // NC
    place = ((l ^ (1 - ll)) * NZ + (z + zz + 1) % NZ) * NC + (k ^ kk)
    column = (place * NY + (y + yy + 1) % NY) * quarter + start + r
    pick = b16(lax.broadcasted_iota(jnp.int32, (n_vir, size), 0) == column)
    return b16(jnp.dot(virt_coeffs, pick, preferred_element_type=jnp.float32))


def placed_rows(done, quarter, start, rows, n_occ):
    y = places()[0]
    size = NY * n_occ * rows
    shape = (NY * quarter * n_occ, size)
    at = lax.broadcasted_iota(jnp.int32, shape, 1)
    r, at = at % rows, at // rows
    i, yy = at % n_occ, at // n_occ
    row = (((y + yy + 1) % NY) * quarter + start + r) * n_occ + i
    place = f32(lax.broadcasted_iota(jnp.int32, shape, 0) == row)
    return jnp.dot(place, done, precision=lax.Precision.HIGHEST, preferred_element_type=jnp.float32)


def partial_sums(half_ints, cols):
    n_occ, _, width = half_ints.shape
    per = cols.shape[1] // NY
    blocks = [
        (lax.dot_general(cols, half_ints[i], (((0,), (0,)), ((), ())), preferred_element_type=jnp.float32) * SCALE)
        .astype(jnp.float16)
        .reshape(NY, per, width)
        for i in range(n_occ)
    ]
    return [jnp.stack([blocks[i][n] for i in range(n_occ)]) for n in range(NY)]


def fit_kernel(near_u, far_u, back_u, mine_u, own, other, near, far, back, mine, rows):
    units = (near_u, far_u, back_u, mine_u)
    n_occ, _, r, _ = mine_u.shape

    @pl.when(pl.program_id(0) == 0)
    def _():
        for n, unit in enumerate(units):
            for i in range(n_occ):
                g = n * n_occ + i
                for h in range(2):
                    rows[h, g * r : (g + 1) * r, :] = unit[i, h]

    by_columns = (((1,), (1,)), ((), ()))
    total = lax.dot_general(rows[0], own[...], by_columns, preferred_element_type=jnp.float32)
    total = total + lax.dot_general(rows[1], other[...], by_columns, preferred_element_type=jnp.float32)
    one = r // NZ
    for z, out in enumerate((near, far, back, mine)):
        groups = [total[g * r + z * one : g * r + (z + 1) * one] for g in range(NY * n_occ)]
        out[...] = jnp.concatenate(groups, 0).astype(out.dtype)


def fit(units, own, other):
    n_occ, _, r, width = units[0].shape
    n_cols = own.shape[0]
    n_rows = NY * n_occ * r
    unit = pl.BlockSpec(units[0].shape, lambda q: (0, 0, 0, 0))
    factor = pl.BlockSpec((TILE, width), lambda q: (q, 0))
    out = pl.BlockSpec((n_rows // NZ, TILE), lambda q: (0, q))
    shape = lambda d: jax.ShapeDtypeStruct((n_rows // NZ, n_cols), d)
    return pl.pallas_call(
        fit_kernel,
        grid=(pl.cdiv(n_cols, TILE),),
        in_specs=[unit] * NY + [factor] * 2,
        out_specs=[out] * NZ,
        out_shape=[shape(jnp.bfloat16)] * 3 + [shape(jnp.float32)],
        scratch_shapes=[pltpu.VMEM((2, n_rows, width), jnp.bfloat16)],
        compiler_params=pltpu.CompilerParams(vmem_limit_bytes=40 << 20),
        cost_estimate=pl.CostEstimate(
            flops=4 * n_rows * width * n_cols, bytes_accessed=4 * width * n_cols + 2 * n_rows * n_cols, transcendentals=0
        ),
    )(*units, own, other)


def on_device(half_ints, virt_coeffs, metric_factor):
    n_occ = half_ints.shape[0]
    n_vir = virt_coeffs.shape[1]
    width = metric_factor.shape[1]
    quarter = n_vir // (NL * NZ * NC * NY)
    starts = [sum(PARTS[:p]) for p in range(len(PARTS))]
    parts = range(len(PARTS))

    sums = [partial_sums(half_ints, picked(virt_coeffs, quarter, starts[p], PARTS[p])) for p in parts]
    other_factor = lax.ppermute(metric_factor, "aux", SWAP_CORE)
    own_t, other_t = metric_factor.T, other_factor.T

    gathered, previous = [], None
    for p in parts:
        near, far, back, mine = sums[p]
        if previous is not None:
            near, far, back = after((near, far, back), previous)
        got = [on_y(near, 1), on_y(back, 3), on_y(far, 2)]
        previous = got
        total = f32(mine) + f32(got[0]) + f32(got[1]) + f32(got[2])
        pair = b16((total + f32(lax.ppermute(total.astype(jnp.float16), "basis", SWAP_H))) * (1 / SCALE))
        keep = pair.shape[1] // NC
        swapped = lax.ppermute(pair[:, keep:], "aux", SWAP_CORE)
        block = jnp.stack([pair[:, :keep], swapped], axis=1)
        gathered.append([on_y(block, 3), on_y(block, 2), on_y(block, 1), block])

    results = []
    for p in parts:
        near, far, back, mine = fit(gathered[p], own_t, other_t)
        total = mine + f32(on_z(near, 1)) + f32(on_z(back, 3)) + f32(on_z(far, 2))
        total = total.reshape(NY * n_occ, NL, PARTS[p], width)
        done = total[:, 1] + f32(lax.ppermute(b16(total[:, 0]), "aux", SWAP_L))
        results.append(placed_rows(done.reshape(-1, width), quarter, starts[p], PARTS[p], n_occ))
    return sum(results[1:], results[0])


def solution(mesh):
    placed = (P(None, "basis", "aux"), P("basis", None), P("aux", "basis"))
    return jax.shard_map(
        on_device, mesh=mesh, in_specs=placed, out_specs=P("aux", "basis"), check_vma=False
    )
```

```python
import jax
import jax.numpy as jnp
from jax import lax
from jax.experimental import pallas as pl
from jax.experimental.layout import Layout, with_layout_constraint
from jax.experimental.pallas import tpu as pltpu
from jax.sharding import PartitionSpec as P

NY, NH, NL, NZ, NC = 4, 2, 2, 4, 2
PARTS = (4, 4, 4)
SCALE = 16.0
TILE = 512

SWAP_H = [(i, i ^ 1) for i in range(NY * NH)]
SWAP_CORE = [(i, i ^ 1) for i in range(NL * NZ * NC)]
SWAP_L = [(i, i ^ (NZ * NC)) for i in range(NL * NZ * NC)]


def swap(x, axis, turn):
    n_aux = NL * NZ * NC
    pairs = []
    for i in range(NY * NH * n_aux):
        y, h, l, z, k = i // n_aux // NH, i // n_aux % NH, i % n_aux // (NZ * NC), i // NC % NZ, i % NC
        mask = 1 if k == turn else 3
        y, z = (y ^ mask, z) if axis == "y" else (y, z ^ mask)
        pairs.append((i, (y * NH + h) * n_aux + (l * NZ + z) * NC + k))
    return permuted(x, ("basis", "aux"), pairs)


def mask_of(slot, core):
    return jnp.where(slot == 0, 2, jnp.where(slot == 1, 1 + 2 * core, jnp.where(slot == 2, 3 - 2 * core, 0)))


def places():
    basis, aux = lax.axis_index("basis"), lax.axis_index("aux")
    return basis // NH, aux // (NZ * NC), aux // NC % NZ, aux % NC


def after(x, earlier):
    return lax.optimization_barrier((x, earlier))[0]


def by_rows(x):
    return with_layout_constraint(x, Layout(major_to_minor=tuple(range(x.ndim))))


def permuted(x, axis, pairs):
    return by_rows(lax.ppermute(by_rows(x), axis, pairs))


def f32(x):
    return x.astype(jnp.float32)


def b16(x):
    return x.astype(jnp.bfloat16)


def picked(virt_coeffs, quarter, start, rows):
    y, l, z, k = places()
    n_vir = virt_coeffs.shape[1]
    size = NY * NC * NZ * NL * rows
    at = lax.broadcasted_iota(jnp.int32, (n_vir, size), 1)
    r, at = at % rows, at // rows
    ll, at = at % NL, at // NL
    zz, at = at % NZ, at // NZ
    kk, yy = at % NC, at // NC
    core = k ^ kk
    place = ((l ^ (1 - ll)) * NZ + (z ^ mask_of(zz, core))) * NC + core
    column = (place * NY + (y ^ mask_of(yy, k))) * quarter + start + r
    pick = b16(lax.broadcasted_iota(jnp.int32, (n_vir, size), 0) == column)
    return b16(jnp.dot(virt_coeffs, pick, preferred_element_type=jnp.float32))


def placed_rows(done, quarter, start, rows, n_occ):
    y, _, _, k = places()
    size = NY * n_occ * rows
    shape = (NY * quarter * n_occ, size)
    at = lax.broadcasted_iota(jnp.int32, shape, 1)
    r, at = at % rows, at // rows
    i, yy = at % n_occ, at // n_occ
    row = ((y ^ mask_of(NY - 1 - yy, k)) * quarter + start + r) * n_occ + i
    place = f32(lax.broadcasted_iota(jnp.int32, shape, 0) == row)
    return jnp.dot(place, done, precision=lax.Precision.HIGHEST, preferred_element_type=jnp.float32)


def partial_sums(half_ints, cols):
    blocks = []
    for half in half_ints:
        block = lax.dot_general(cols, half, (((0,), (0,)), ((), ())), preferred_element_type=jnp.float32)
        blocks.append(by_rows((block * SCALE).astype(jnp.float16)))
    n_rows, width = blocks[0].shape
    halves = [block.reshape(2, 2, n_rows // NY, width) for block in blocks]
    return by_rows(jnp.stack([half[0] for half in halves])), by_rows(jnp.stack([half[1] for half in halves]))


def swapped_factor(factor):
    return lax.ppermute(factor, "aux", SWAP_CORE)


def fit_kernel(near, far, own, other, away, keep, rows):
    n_unit, n_occ, _, r, _ = near.shape

    @pl.when(pl.program_id(0) == 0)
    def _():
        for n, units in enumerate((near, far)):
            for u in range(n_unit):
                for i in range(n_occ):
                    g = (n * n_unit + u) * n_occ + i
                    for h in range(2):
                        rows[h, g * r : (g + 1) * r, :] = units[u, i, h]

    by_columns = (((1,), (1,)), ((), ()))
    total = lax.dot_general(rows[0], own[...], by_columns, preferred_element_type=jnp.float32)
    total = total + lax.dot_general(rows[1], other[...], by_columns, preferred_element_type=jnp.float32)
    one = r // (NZ * NL)
    for z in range(NZ):
        out = away if z < NZ // 2 else keep
        first = [g * r + (z * NL + l) * one for l in range(NL) for g in range(NY * n_occ)]
        out[0, z % (NZ // 2)] = jnp.concatenate([total[f : f + one] for f in first], 0).astype(out.dtype)


def fit(near, far, own, other):
    n_unit, n_occ, _, r, width = near.shape
    n_cols = own.shape[0]
    n_rows = 2 * n_unit * n_occ * r
    units = pl.BlockSpec(near.shape, lambda q: (0, 0, 0, 0, 0))
    factor = pl.BlockSpec((TILE, width), lambda q: (q, 0))
    out = pl.BlockSpec((1, NZ // 2, n_rows // NZ, TILE), lambda q: (0, 0, 0, q))
    shape = lambda d: jax.ShapeDtypeStruct((1, NZ // 2, n_rows // NZ, n_cols), d)
    return pl.pallas_call(
        fit_kernel,
        grid=(pl.cdiv(n_cols, TILE),),
        in_specs=[units] * 2 + [factor] * 2,
        out_specs=[out] * 2,
        out_shape=[shape(jnp.bfloat16), shape(jnp.float32)],
        scratch_shapes=[pltpu.VMEM((2, n_rows, width), jnp.bfloat16)],
        compiler_params=pltpu.CompilerParams(vmem_limit_bytes=40 << 20),
        cost_estimate=pl.CostEstimate(
            flops=4 * n_rows * width * n_cols,
            bytes_accessed=4 * width * n_cols + 3 * n_rows * n_cols,
            transcendentals=0,
        ),
    )(near, far, own, other)


class Part:
    def __init__(self, away, keep):
        self.away, self.keep = away, keep

    def sum_y(self, *ready):
        got = swap(after(self.away, ready), "y", 0)
        self.kept = f32(self.keep) + f32(got)

    def sum_y_again(self, *ready):
        got = swap(self.kept[:, 0].astype(jnp.float16), "y", 1)
        self.total = after(self.kept[:, 1], ready) + f32(got)

    def sum_h(self, *ready):
        got = permuted(self.total.astype(jnp.float16), "basis", SWAP_H)
        pair = b16((after(self.total, ready) + f32(got)) * (1 / SCALE))
        middle = pair.shape[1] // NC
        got = permuted(pair[:, middle:], "aux", SWAP_CORE)
        self.block = by_rows(jnp.stack([pair[:, :middle], got], axis=1))

    def gather_y(self, *ready):
        got = swap(self.block, "y", 1)
        self.near = by_rows(jnp.stack([after(self.block, ready), got]))

    def gather_y_again(self):
        self.far = swap(self.near, "y", 0)

    def fit(self, own, other, *ready):
        self.away, self.keep = fit(after(self.near, ready), self.far, own, other)

    def sum_z(self, *ready):
        got = swap(self.away, "z", 0)
        self.kept = after(self.keep, ready) + f32(got)

    def sum_z_again(self, *ready):
        got = swap(b16(self.kept[:, 0]), "z", 1)
        self.total = (after(self.kept[:, 1], ready) + f32(got))[0]

    def sum_l(self, *ready):
        middle = self.total.shape[0] // NL
        got = permuted(b16(self.total[:middle]), "aux", SWAP_L)
        self.done = after(self.total[middle:], ready) + f32(got)


def on_device(half_ints, virt_coeffs, metric_factor):
    n_occ = half_ints.shape[0]
    n_vir = virt_coeffs.shape[1]
    quarter = n_vir // (NL * NZ * NC * NY)
    starts = [sum(PARTS[:p]) for p in range(len(PARTS))]
    parts = range(len(PARTS))
    first, second, third = [
        Part(*partial_sums(half_ints, picked(virt_coeffs, quarter, starts[p], PARTS[p]))) for p in parts
    ]
    other = swapped_factor(metric_factor).T
    own = metric_factor.T
    first.sum_y()
    second.sum_y(first.kept)
    third.sum_y(second.kept)
    for part in (first, second, third):
        part.sum_y_again()
    first.sum_h()
    second.sum_h(third.kept, first.block)
    third.sum_h()
    first.gather_y()
    second.gather_y()
    for part in (first, second):
        part.gather_y_again()
    first.fit(own, other)
    third.gather_y(first.keep)
    third.gather_y_again()
    second.fit(own, other, third.near)
    third.fit(own, other)
    for part in (first, second, third):
        part.sum_z()
        part.sum_z_again()
        part.sum_l()
    done = [
        placed_rows(part.done, quarter, starts[p], PARTS[p], n_occ) for p, part in enumerate((first, second, third))
    ]
    return sum(done[1:], done[0])


def solution(mesh):
    placed = (P(None, "basis", "aux"), P("basis", None), P("aux", "basis"))
    return jax.shard_map(
        on_device, mesh=mesh, in_specs=placed, out_specs=P("aux", "basis"), check_vma=False
    )
```

```python
import jax
import jax.numpy as jnp
from jax import lax
from jax.experimental import pallas as pl
from jax.experimental.layout import Layout, with_layout_constraint
from jax.experimental.pallas import tpu as pltpu
from jax.sharding import PartitionSpec as P

NY, NH, NL, NZ, NC = 4, 2, 2, 4, 2
PARTS = (4, 4, 4)
SCALE = 16.0
TILE = 512

SWAP_H = [(i, i ^ 1) for i in range(NY * NH)]
SWAP_CORE = [(i, i ^ 1) for i in range(NL * NZ * NC)]
SWAP_L = [(i, i ^ (NZ * NC)) for i in range(NL * NZ * NC)]


def swap(x, axis, turn):
    n_aux = NL * NZ * NC
    pairs = []
    for i in range(NY * NH * n_aux):
        y, h, l, z, k = i // n_aux // NH, i // n_aux % NH, i % n_aux // (NZ * NC), i // NC % NZ, i % NC
        mask = 1 if k == turn else 3
        y, z = (y ^ mask, z) if axis == "y" else (y, z ^ mask)
        pairs.append((i, (y * NH + h) * n_aux + (l * NZ + z) * NC + k))
    return permuted(x, ("basis", "aux"), pairs)


def mask_of(slot, core):
    return jnp.where(slot == 0, 2, jnp.where(slot == 1, 1 + 2 * core, jnp.where(slot == 2, 3 - 2 * core, 0)))


def places():
    basis, aux = lax.axis_index("basis"), lax.axis_index("aux")
    return basis // NH, aux // (NZ * NC), aux // NC % NZ, aux % NC


def after(x, earlier):
    return lax.optimization_barrier((x, earlier))[0]


def by_rows(x):
    return with_layout_constraint(x, Layout(major_to_minor=tuple(range(x.ndim))))


def permuted(x, axis, pairs):
    return by_rows(lax.ppermute(by_rows(x), axis, pairs))


def f32(x):
    return x.astype(jnp.float32)


def b16(x):
    return x.astype(jnp.bfloat16)


def picked(virt_coeffs, quarter, start, rows):
    y, l, z, k = places()
    n_vir = virt_coeffs.shape[1]
    size = NY * NC * NZ * NL * rows
    at = lax.broadcasted_iota(jnp.int32, (n_vir, size), 1)
    r, at = at % rows, at // rows
    ll, at = at % NL, at // NL
    zz, at = at % NZ, at // NZ
    kk, yy = at % NC, at // NC
    core = k ^ kk
    place = ((l ^ (1 - ll)) * NZ + (z ^ mask_of(zz, core))) * NC + core
    column = (place * NY + (y ^ mask_of(yy, k))) * quarter + start + r
    pick = b16(lax.broadcasted_iota(jnp.int32, (n_vir, size), 0) == column)
    return b16(jnp.dot(virt_coeffs, pick, preferred_element_type=jnp.float32))


def placed_rows(done, quarter, start, rows, n_occ):
    y, _, _, k = places()
    size = NY * n_occ * rows
    shape = (NY * quarter * n_occ, size)
    at = lax.broadcasted_iota(jnp.int32, shape, 1)
    r, at = at % rows, at // rows
    i, yy = at % n_occ, at // n_occ
    row = ((y ^ mask_of(NY - 1 - yy, k)) * quarter + start + r) * n_occ + i
    place = f32(lax.broadcasted_iota(jnp.int32, shape, 0) == row)
    return jnp.dot(place, done, precision=lax.Precision.HIGHEST, preferred_element_type=jnp.float32)


def partial_sums(half_ints, cols):
    blocks = []
    for half in half_ints:
        block = lax.dot_general(cols, half, (((0,), (0,)), ((), ())), preferred_element_type=jnp.float32)
        blocks.append(by_rows((block * SCALE).astype(jnp.float16)))
    n_rows, width = blocks[0].shape
    halves = [block.reshape(2, 2, n_rows // NY, width) for block in blocks]
    return by_rows(jnp.stack([half[0] for half in halves])), by_rows(jnp.stack([half[1] for half in halves]))


def swapped_factor(factor):
    return lax.ppermute(factor, "aux", SWAP_CORE)


def fit_kernel(near, far, own, other, away, keep, rows):
    n_unit, n_occ, _, r, _ = near.shape

    @pl.when(pl.program_id(0) == 0)
    def _():
        for n, units in enumerate((near, far)):
            for u in range(n_unit):
                for i in range(n_occ):
                    g = (n * n_unit + u) * n_occ + i
                    for h in range(2):
                        rows[h, g * r : (g + 1) * r, :] = units[u, i, h]

    by_columns = (((1,), (1,)), ((), ()))
    total = lax.dot_general(rows[0], own[...], by_columns, preferred_element_type=jnp.float32)
    total = total + lax.dot_general(rows[1], other[...], by_columns, preferred_element_type=jnp.float32)
    one = r // (NZ * NL)
    for z in range(NZ):
        out = away if z < NZ // 2 else keep
        first = [g * r + (z * NL + l) * one for l in range(NL) for g in range(NY * n_occ)]
        out[0, z % (NZ // 2)] = jnp.concatenate([total[f : f + one] for f in first], 0).astype(out.dtype)


def fit(near, far, own, other):
    n_unit, n_occ, _, r, width = near.shape
    n_cols = own.shape[0]
    n_rows = 2 * n_unit * n_occ * r
    units = pl.BlockSpec(near.shape, lambda q: (0, 0, 0, 0, 0))
    factor = pl.BlockSpec((TILE, width), lambda q: (q, 0))
    out = pl.BlockSpec((1, NZ // 2, n_rows // NZ, TILE), lambda q: (0, 0, 0, q))
    shape = lambda d: jax.ShapeDtypeStruct((1, NZ // 2, n_rows // NZ, n_cols), d)
    return pl.pallas_call(
        fit_kernel,
        grid=(pl.cdiv(n_cols, TILE),),
        in_specs=[units] * 2 + [factor] * 2,
        out_specs=[out] * 2,
        out_shape=[shape(jnp.bfloat16), shape(jnp.float32)],
        scratch_shapes=[pltpu.VMEM((2, n_rows, width), jnp.bfloat16)],
        compiler_params=pltpu.CompilerParams(vmem_limit_bytes=40 << 20),
        cost_estimate=pl.CostEstimate(
            flops=4 * n_rows * width * n_cols,
            bytes_accessed=4 * width * n_cols + 3 * n_rows * n_cols,
            transcendentals=0,
        ),
    )(near, far, own, other)


class Part:
    def __init__(self, away, keep):
        self.away, self.keep = away, keep

    def sum_y(self, *ready):
        got = swap(after(self.away, ready), "y", 0)
        self.kept = f32(self.keep) + f32(got)

    def sum_y_again(self, *ready):
        got = swap(self.kept[:, 0].astype(jnp.float16), "y", 1)
        self.total = after(self.kept[:, 1], ready) + f32(got)

    def sum_h(self, *ready):
        got = permuted(self.total.astype(jnp.float16), "basis", SWAP_H)
        pair = b16((after(self.total, ready) + f32(got)) * (1 / SCALE))
        middle = pair.shape[1] // NC
        got = permuted(pair[:, middle:], "aux", SWAP_CORE)
        self.block = by_rows(jnp.stack([pair[:, :middle], got], axis=1))

    def gather_y(self, *ready):
        got = swap(self.block, "y", 1)
        self.near = by_rows(jnp.stack([after(self.block, ready), got]))

    def gather_y_again(self):
        self.far = swap(self.near, "y", 0)

    def fit(self, own, other, *ready):
        self.away, self.keep = fit(after(self.near, ready), self.far, own, other)

    def sum_z(self, *ready):
        got = swap(self.away, "z", 0)
        self.kept = after(self.keep, ready) + f32(got)

    def sum_z_again(self, *ready):
        got = swap(b16(self.kept[:, 0]), "z", 1)
        self.total = (after(self.kept[:, 1], ready) + f32(got))[0]

    def sum_l(self, *ready):
        middle = self.total.shape[0] // NL
        got = permuted(b16(self.total[:middle]), "aux", SWAP_L)
        self.done = after(self.total[middle:], ready) + f32(got)


def on_device(half_ints, virt_coeffs, metric_factor):
    n_occ = half_ints.shape[0]
    n_vir = virt_coeffs.shape[1]
    quarter = n_vir // (NL * NZ * NC * NY)
    starts = [sum(PARTS[:p]) for p in range(len(PARTS))]
    parts = range(len(PARTS))
    first, second, third = [
        Part(*partial_sums(half_ints, picked(virt_coeffs, quarter, starts[p], PARTS[p]))) for p in parts
    ]
    other = swapped_factor(metric_factor).T
    own = metric_factor.T
    first.sum_y()
    second.sum_y(first.kept)
    third.sum_y(second.kept)
    for part in (first, second, third):
        part.sum_y_again()
    first.sum_h()
    second.sum_h(third.kept, first.block)
    third.sum_h()
    first.gather_y()
    second.gather_y(other)
    for part in (first, second):
        part.gather_y_again()
    first.fit(own, other)
    third.gather_y(first.keep)
    third.gather_y_again()
    second.fit(own, other)
    third.fit(own, other)
    first.sum_z()
    third.sum_z()
    second.sum_z(third.kept)
    for part in (first, second, third):
        part.sum_z_again()
        part.sum_l()
    done = [
        placed_rows(part.done, quarter, starts[p], PARTS[p], n_occ) for p, part in enumerate((first, second, third))
    ]
    return sum(done[1:], done[0])


def solution(mesh):
    placed = (P(None, "basis", "aux"), P("basis", None), P("aux", "basis"))
    return jax.shard_map(
        on_device, mesh=mesh, in_specs=placed, out_specs=P("aux", "basis"), check_vma=False
    )
```

```python
import jax
import jax.numpy as jnp
from jax import lax
from jax.experimental import pallas as pl
from jax.experimental.layout import Layout, with_layout_constraint
from jax.experimental.pallas import tpu as pltpu
from jax.sharding import PartitionSpec as P

NY, NH, NL, NZ, NC = 4, 2, 2, 4, 2
PARTS = (4, 4, 4)
SCALE = 16.0
TILE = 768

SWAP_H = [(i, i ^ 1) for i in range(NY * NH)]
SWAP_CORE = [(i, i ^ 1) for i in range(NL * NZ * NC)]
SWAP_L = [(i, i ^ (NZ * NC)) for i in range(NL * NZ * NC)]


def swap(x, axis, turn):
    n_aux = NL * NZ * NC
    pairs = []
    for i in range(NY * NH * n_aux):
        y, h, l, z, k = i // n_aux // NH, i // n_aux % NH, i % n_aux // (NZ * NC), i // NC % NZ, i % NC
        mask = 1 if k == turn else 3
        y, z = (y ^ mask, z) if axis == "y" else (y, z ^ mask)
        pairs.append((i, (y * NH + h) * n_aux + (l * NZ + z) * NC + k))
    return permuted(x, ("basis", "aux"), pairs)


def mask_of(slot, core):
    return jnp.where(slot == 0, 2, jnp.where(slot == 1, 1 + 2 * core, jnp.where(slot == 2, 3 - 2 * core, 0)))


def places():
    basis, aux = lax.axis_index("basis"), lax.axis_index("aux")
    return basis // NH, aux // (NZ * NC), aux // NC % NZ, aux % NC


def after(x, earlier):
    return lax.optimization_barrier((x, earlier))[0]


def by_rows(x):
    return with_layout_constraint(x, Layout(major_to_minor=tuple(range(x.ndim))))


def permuted(x, axis, pairs):
    return by_rows(lax.ppermute(by_rows(x), axis, pairs))


def f32(x):
    return x.astype(jnp.float32)


def b16(x):
    return x.astype(jnp.bfloat16)


def picked(virt_coeffs, quarter, start, rows):
    y, l, z, k = places()
    n_vir = virt_coeffs.shape[1]
    size = NY * NC * NZ * NL * rows
    at = lax.broadcasted_iota(jnp.int32, (n_vir, size), 1)
    r, at = at % rows, at // rows
    ll, at = at % NL, at // NL
    zz, at = at % NZ, at // NZ
    kk, yy = at % NC, at // NC
    core = k ^ kk
    place = ((l ^ (1 - ll)) * NZ + (z ^ mask_of(zz, core))) * NC + core
    column = (place * NY + (y ^ mask_of(yy, k))) * quarter + start + r
    pick = b16(lax.broadcasted_iota(jnp.int32, (n_vir, size), 0) == column)
    return b16(jnp.dot(virt_coeffs, pick, preferred_element_type=jnp.float32))


def placed_rows(done, quarter, start, rows, n_occ):
    y, _, _, k = places()
    size = NY * n_occ * rows
    shape = (NY * quarter * n_occ, size)
    at = lax.broadcasted_iota(jnp.int32, shape, 1)
    r, at = at % rows, at // rows
    i, yy = at % n_occ, at // n_occ
    row = ((y ^ mask_of(NY - 1 - yy, k)) * quarter + start + r) * n_occ + i
    place = f32(lax.broadcasted_iota(jnp.int32, shape, 0) == row)
    return jnp.dot(place, done, precision=lax.Precision.HIGHEST, preferred_element_type=jnp.float32)


def partial_sums(half_ints, cols):
    blocks = []
    for half in half_ints:
        block = lax.dot_general(cols, half, (((0,), (0,)), ((), ())), preferred_element_type=jnp.float32)
        blocks.append(by_rows((block * SCALE).astype(jnp.float16)))
    n_rows, width = blocks[0].shape
    halves = [block.reshape(2, 2, n_rows // NY, width) for block in blocks]
    return by_rows(jnp.stack([half[0] for half in halves])), by_rows(jnp.stack([half[1] for half in halves]))


def swapped_factor(factor):
    return lax.ppermute(factor, "aux", SWAP_CORE)


def fit_kernel(near, far, own, other, away, keep, rows):
    n_unit, n_occ, _, r, _ = near.shape

    @pl.when(pl.program_id(0) == 0)
    def _():
        for n, units in enumerate((near, far)):
            for u in range(n_unit):
                for i in range(n_occ):
                    g = (n * n_unit + u) * n_occ + i
                    for h in range(2):
                        rows[h, g * r : (g + 1) * r, :] = units[u, i, h]

    by_columns = (((1,), (1,)), ((), ()))
    total = lax.dot_general(rows[0], own[...], by_columns, preferred_element_type=jnp.float32)
    total = total + lax.dot_general(rows[1], other[...], by_columns, preferred_element_type=jnp.float32)
    one = r // (NZ * NL)
    for z in range(NZ):
        out = away if z < NZ // 2 else keep
        first = [g * r + (z * NL + l) * one for l in range(NL) for g in range(NY * n_occ)]
        out[0, z % (NZ // 2)] = jnp.concatenate([total[f : f + one] for f in first], 0).astype(out.dtype)


def fit(near, far, own, other):
    n_unit, n_occ, _, r, width = near.shape
    n_cols = own.shape[0]
    n_rows = 2 * n_unit * n_occ * r
    units = pl.BlockSpec(near.shape, lambda q: (0, 0, 0, 0, 0))
    factor = pl.BlockSpec((TILE, width), lambda q: (q, 0))
    out = pl.BlockSpec((1, NZ // 2, n_rows // NZ, TILE), lambda q: (0, 0, 0, q))
    shape = lambda d: jax.ShapeDtypeStruct((1, NZ // 2, n_rows // NZ, n_cols), d)
    return pl.pallas_call(
        fit_kernel,
        grid=(pl.cdiv(n_cols, TILE),),
        in_specs=[units] * 2 + [factor] * 2,
        out_specs=[out] * 2,
        out_shape=[shape(jnp.bfloat16), shape(jnp.float32)],
        scratch_shapes=[pltpu.VMEM((2, n_rows, width), jnp.bfloat16)],
        compiler_params=pltpu.CompilerParams(vmem_limit_bytes=40 << 20),
        cost_estimate=pl.CostEstimate(
            flops=4 * n_rows * width * n_cols,
            bytes_accessed=4 * width * n_cols + 3 * n_rows * n_cols,
            transcendentals=0,
        ),
    )(near, far, own, other)


class Part:
    def __init__(self, away, keep):
        self.away, self.keep = away, keep

    def sum_y(self, *ready):
        got = swap(after(self.away, ready), "y", 0)
        self.kept = f32(self.keep) + f32(got)

    def sum_y_again(self, *ready):
        got = swap(self.kept[:, 0].astype(jnp.float16), "y", 1)
        self.total = after(self.kept[:, 1], ready) + f32(got)

    def sum_h(self, *ready):
        got = permuted(self.total.astype(jnp.float16), "basis", SWAP_H)
        pair = b16((after(self.total, ready) + f32(got)) * (1 / SCALE))
        middle = pair.shape[1] // NC
        got = permuted(pair[:, middle:], "aux", SWAP_CORE)
        self.block = by_rows(jnp.stack([pair[:, :middle], got], axis=1))

    def gather_y(self, *ready):
        got = swap(self.block, "y", 1)
        self.near = by_rows(jnp.stack([after(self.block, ready), got]))

    def gather_y_again(self):
        self.far = swap(self.near, "y", 0)

    def fit(self, own, other, *ready):
        self.away, self.keep = fit(after(self.near, ready), self.far, own, other)

    def sum_z(self, *ready):
        got = swap(self.away, "z", 0)
        self.kept = after(self.keep, ready) + f32(got)

    def sum_z_again(self, *ready):
        got = swap(b16(self.kept[:, 0]), "z", 1)
        self.total = (after(self.kept[:, 1], ready) + f32(got))[0]

    def sum_l(self, *ready):
        middle = self.total.shape[0] // NL
        got = permuted(b16(self.total[:middle]), "aux", SWAP_L)
        self.done = after(self.total[middle:], ready) + f32(got)


def on_device(half_ints, virt_coeffs, metric_factor):
    n_occ = half_ints.shape[0]
    n_vir = virt_coeffs.shape[1]
    quarter = n_vir // (NL * NZ * NC * NY)
    starts = [sum(PARTS[:p]) for p in range(len(PARTS))]
    parts = range(len(PARTS))
    first, second, third = [
        Part(*partial_sums(half_ints, picked(virt_coeffs, quarter, starts[p], PARTS[p]))) for p in parts
    ]
    other = swapped_factor(metric_factor).T
    own = metric_factor.T
    first.sum_y()
    second.sum_y(first.kept)
    third.sum_y(second.kept)
    for part in (first, second, third):
        part.sum_y_again()
    first.sum_h()
    second.sum_h(third.kept, first.block)
    third.sum_h()
    first.gather_y()
    second.gather_y(other)
    for part in (first, second):
        part.gather_y_again()
    first.fit(own, other)
    third.gather_y(first.keep)
    third.gather_y_again()
    second.fit(own, other)
    third.fit(own, other)
    first.sum_z()
    third.sum_z()
    second.sum_z(third.kept)
    for part in (first, second, third):
        part.sum_z_again()
        part.sum_l()
    done = [
        placed_rows(part.done, quarter, starts[p], PARTS[p], n_occ) for p, part in enumerate((first, second, third))
    ]
    return sum(done[1:], done[0])


def solution(mesh):
    placed = (P(None, "basis", "aux"), P("basis", None), P("aux", "basis"))
    return jax.shard_map(
        on_device, mesh=mesh, in_specs=placed, out_specs=P("aux", "basis"), check_vma=False
    )
```
